32 devices in a mesh: gx: 8 (over z, y), gy: 4 (over x, core).
Axes of the slice: x: 2, y: 2, z: 4, core: 2. Of those that a mesh axis runs over, the one named last changes fastest.
Arguments:
- vorticity: float32 [8192, 8192], P('gx', 'gy'), may hold values from -6 to 6
- closure_kernel: float32 [3, 3, 3], replicated, may hold values from -1.5 to 1.5
Outputs:
- rate_field: float32 [8192, 8192], P('gx', 'gy')
The draws below stay inside these ranges and needn't reach their ends.
All inputs are finite; a program needn't handle non-finite values.
Results may differ from the reference program's by a relative error of at most 0.0001.
Values sent between devices are 32-bit elements; how exact they have to be, the bound alone decides.
A program may use at most 256 MiB of HBM per device.

```python
import math
import jax
import jax.numpy as jnp

GRID = 8192


def draw_vorticity(key, part):
    rough_part = jax.random.normal(key, (GRID, GRID), jnp.float32)
    return jnp.clip(rough_part, -6.0, 6.0)


def bell_draw(stream_key, dims, width, most, dtype=jnp.bfloat16):
    values = jax.random.normal(stream_key, dims, jnp.float32) * width
    return jnp.minimum(jnp.maximum(values, -most), most).astype(dtype)


def setup_inputs(seed: int = 0) -> dict:
    arg_keys = jax.random.split(jax.random.key(seed), 3)
    return {
        "vorticity": draw_vorticity(jax.random.fold_in(arg_keys[2], 71), 0),
        "closure_kernel": bell_draw(arg_keys[1], (3, 3, 3), 0.3, 1.5, jnp.float32),
    }


VISCOSITY = 0.5
DRAG = 0.1
FORCE_AMP = 1.0
FORCE_WAVES = 4.0


def transform_speeds(field):
    half_length = GRID // 2
    spectrum = jnp.fft.rfft(field, axis=1)[:, :half_length]
    spectrum = jnp.fft.fft(spectrum, axis=0)
    index_first = jnp.arange(GRID)
    index_first = jnp.where(index_first < half_length, index_first, index_first - GRID)
    number_first = (2.0 * math.pi / GRID) * index_first.astype(jnp.float32)
    number_second = (2.0 * math.pi / GRID) * jnp.arange(half_length).astype(jnp.float32)
    squared = number_first[:, None] ** 2 + number_second[None, :] ** 2
    positive = squared > 0.0
    inverse = jnp.where(positive, 1.0 / jnp.where(positive, squared, 1.0), 0.0)
    potential = spectrum * inverse
    along = 1j * number_second[None, :] * potential
    across = -1j * number_first[:, None] * potential
    speeds = []
    for spectral in (along, across):
        mixed = jnp.fft.ifft(spectral, axis=0)
        mixed = mixed.at[:, 0].set(jnp.real(mixed[:, 0]))
        mixed = jnp.pad(mixed, ((0, 0), (0, 1)))
        speeds.append(jnp.fft.irfft(mixed, n=GRID, axis=1))
    return speeds[0], speeds[1]


def shifted(array, rows_by, cols_by):
    return jnp.roll(array, (rows_by, cols_by), axis=(0, 1))


def rate_of(field, closure_kernel):
    speed_first, speed_second = transform_speeds(field)
    x_minus = shifted(field, 1, 0)
    x_plus = shifted(field, -1, 0)
    y_minus = shifted(field, 0, 1)
    y_plus = shifted(field, 0, -1)
    advect = jnp.maximum(speed_first, 0.0) * (field - x_minus) + jnp.minimum(speed_first, 0.0) * (x_plus - field)
    advect = advect + jnp.maximum(speed_second, 0.0) * (field - y_minus) + jnp.minimum(speed_second, 0.0) * (y_plus - field)
    laplace = x_plus + x_minus + y_plus + y_minus - 4.0 * field
    closure = jnp.zeros_like(field)
    sources = (field, speed_first, speed_second)
    for channel in range(3):
        for shift_row in range(3):
            for shift_col in range(3):
                closure = closure + closure_kernel[channel, shift_row, shift_col] * shifted(sources[channel], 1 - shift_row, 1 - shift_col)
    columns = jnp.arange(GRID).astype(jnp.float32)
    forcing = FORCE_AMP * jnp.cos((2.0 * math.pi * FORCE_WAVES / GRID) * columns)
    return -advect + VISCOSITY * laplace - DRAG * field + forcing[None, :] + closure


def reference(vorticity, closure_kernel):
    return rate_of(vorticity, closure_kernel)
```

```python
import functools
import math

import jax
import jax.numpy as jnp
import numpy as np
from jax import lax
from jax.experimental import pallas as pl
from jax.experimental.pallas import tpu as pltpu
from jax.sharding import PartitionSpec as P

VISCOSITY = 0.5
DRAG = 0.1
FORCE_AMP = 1.0
FORCE_WAVES = 4.0
TAIL = 64
NEAR = lax.Precision.HIGH
BOTH = ("gx", "gy")


def turns(period, *indices):
    product = functools.reduce(lambda a, b: a * b, np.ix_(*indices)) % period
    return np.exp(2j * np.pi / period * product)


def real_form(table, out_axis, in_axis):
    rows = [
        np.stack([table.real, -table.imag], axis=in_axis),
        np.stack([table.imag, table.real], axis=in_axis),
    ]
    return np.stack(rows, axis=out_axis).astype(np.float32)


def head_forward(lead):
    return real_form(turns(lead, np.arange(lead), np.arange(lead)).conj(), 1, 1)


def tail_forward(length, lead, kept):
    tail = length // lead
    c, b, d = np.arange(lead), np.arange(tail), np.arange(kept)
    table = turns(tail, d, b)[None] * turns(length, c, b)[:, None, :]
    real = real_form(table.conj(), 1, 2)
    return real.reshape(lead, 2 * kept, 2 * tail)


def tail_inverse(length, lead, weights):
    tail = length // lead
    c, b, d = np.arange(lead), np.arange(tail), np.arange(weights.shape[1])
    table = turns(tail, b, d)[None] * turns(length, c, b)[:, :, None] * weights[:, None, :]
    real = real_form(table, 1, 2)
    return real.reshape(lead, 2 * tail, 2 * weights.shape[1])


def head_product(table, cells):
    return jnp.einsum("rh,hbk->rbk", table, cells, precision=NEAR)


def tail_product(table, cells):
    return jnp.einsum("cmn,cnk->cmk", table, cells, precision=NEAR)


def stencil_kernel(grid_length, weights, *refs):
    out_ref = refs[-1]
    rows = out_ref.shape[0]
    fields = [refs[3 * i : 3 * i + 3] for i in range(3)]
    halo = jnp.concatenate([ref[...] for ref in refs[9:12]], axis=0)
    turned = [None, None, None]
    shifted = []
    for channel in range(3):
        mid, before, after = fields[channel]
        centre = jnp.concatenate([before[...], mid[...], after[...]], axis=0)
        minus = jnp.concatenate([halo[:, 2 * channel : 2 * channel + 1], centre[:, :-1]], axis=1)
        plus = jnp.concatenate([centre[:, 1:], halo[:, 2 * channel + 1 : 2 * channel + 2]], axis=1)
        trio = (minus, centre, plus)
        shifted.append(trio)
        for shift_second in range(3):
            for shift_first in range(3):
                term = weights[channel * 9 + shift_first * 3 + shift_second] * trio[shift_first]
                known = turned[shift_second]
                turned[shift_second] = term if known is None else known + term
    closure = turned[0][7 : 7 + rows] + turned[1][8 : 8 + rows] + turned[2][9 : 9 + rows]
    x_minus, whole, x_plus = shifted[0]
    x_minus, x_plus = x_minus[8 : 8 + rows], x_plus[8 : 8 + rows]
    centre = whole[8 : 8 + rows]
    y_minus, y_plus = whole[7 : 7 + rows], whole[9 : 9 + rows]
    first, second = fields[1][0][...], fields[2][0][...]
    advect = jnp.maximum(first, 0.0) * (centre - x_minus) + jnp.minimum(first, 0.0) * (x_plus - centre)
    advect += jnp.maximum(second, 0.0) * (centre - y_minus) + jnp.minimum(second, 0.0) * (y_plus - centre)
    laplace = x_plus + x_minus + y_plus + y_minus - 4.0 * centre
    force = refs[12][...]
    out_ref[...] = closure - advect + VISCOSITY * laplace - DRAG * centre + force


def stencil(field, first, second, halo, force, closure_kernel):
    length, width = field.shape
    rows = 128
    steps = rows // 8
    last = length // 8

    def specs(columns):
        return [
            pl.BlockSpec((rows, columns), lambda i: (i, 0)),
            pl.BlockSpec((8, columns), lambda i: ((i * steps + last - 1) % last, 0)),
            pl.BlockSpec((8, columns), lambda i: ((i * steps + steps) % last, 0)),
        ]

    halo_specs = specs(halo.shape[1])

    def body(weights_ref, *refs):
        weights = [weights_ref[i] for i in range(27)]
        stencil_kernel(length, weights, *refs)

    return pl.pallas_call(
        body,
        grid=(length // rows,),
        in_specs=[pl.BlockSpec(memory_space=pltpu.SMEM)]
        + specs(width) * 3
        + [halo_specs[1], halo_specs[0], halo_specs[2]]
        + [pl.BlockSpec((rows, 1), lambda i: (i, 0))],
        out_specs=pl.BlockSpec((rows, width), lambda i: (i, 0)),
        out_shape=jax.ShapeDtypeStruct((length, width), jnp.float32),
        compiler_params=pltpu.CompilerParams(vmem_limit_bytes=32 * 1024 * 1024),
    )(closure_kernel.reshape(27), *([field] * 3), *([first] * 3), *([second] * 3), *([halo] * 3), force)


def edges(cells):
    count = lax.axis_size("gx") * lax.axis_size("gy")
    onward = [(i, (i + 1) % count) for i in range(count)]
    backward = [((i + 1) % count, i) for i in range(count)]
    from_left = lax.ppermute(cells[..., -1], BOTH, onward)
    from_right = lax.ppermute(cells[..., 0], BOTH, backward)
    return from_left, from_right


def per_device(vorticity, closure_kernel):
    parts = lax.axis_size("gy")
    devices = lax.axis_size("gx") * parts
    rows, columns = vorticity.shape
    length = columns * parts
    width = rows // parts
    tail = min(TAIL, width)
    lead = length // tail
    half = tail // 2
    bands = lead // devices
    waves = bands * half
    folds = width // tail

    turned = vorticity.reshape(parts, width, columns).swapaxes(1, 2)
    field = lax.all_to_all(turned, "gy", 0, 0).reshape(length, width)

    head = head_forward(lead)
    section = head_product(
        head[:, :, 0, :].reshape(2 * lead, lead), field.reshape(lead, tail, width)
    )
    section = tail_product(
        tail_forward(length, lead, half), section.reshape(lead, 2 * tail, width)
    )
    section = section.reshape(devices, bands, 2, half, width).transpose(0, 2, 4, 1, 3)
    lines = lax.all_to_all(section.reshape(devices, 2, width, waves), BOTH, 0, 0)

    mixed = head.reshape(lead, 2, 2, devices, folds).transpose(0, 1, 3, 2, 4)
    wave = head_product(
        mixed.reshape(2 * lead, 2 * lead), lines.reshape(2 * lead, tail, waves)
    )
    wave = tail_product(
        tail_forward(length, lead, tail), wave.reshape(lead, 2 * tail, waves)
    ).reshape(lead, 2, tail, waves)

    unit = 2.0 * math.pi / length
    mode = np.arange(lead)[:, None] + lead * np.arange(tail)[None, :]
    mode = np.where(mode < length // 2, mode, mode - length)
    number_first = jnp.asarray(unit * mode, jnp.float32)[:, :, None]
    local = lax.axis_index(BOTH) * bands + jnp.arange(waves, dtype=jnp.int32) // half
    number_second = unit * (local + lead * (jnp.arange(waves, dtype=jnp.int32) % half)).astype(jnp.float32)
    squared = number_first**2 + number_second**2
    positive = squared > 0.0
    inverse = jnp.where(positive, 1.0 / jnp.where(positive, squared, 1.0), 0.0)
    potential = wave * inverse[:, None]
    spectral = jnp.concatenate(
        [potential * number_second, potential * -number_first[:, None]], axis=-1
    )

    even = np.full((lead, tail), 1.0 / length)
    back = tail_product(
        tail_inverse(length, lead, even), spectral.reshape(lead, 2 * tail, 2 * waves)
    )
    head_back = head.reshape(lead, 2, 2, lead).transpose(3, 2, 0, 1)
    mixed_back = head_back.reshape(devices, folds, 2, lead, 2).transpose(0, 2, 1, 3, 4)
    back = head_product(
        mixed_back.reshape(2 * lead, 2 * lead), back.reshape(2 * lead, tail, 2 * waves)
    )
    lines = lax.all_to_all(back.reshape(devices, 2, width, 2 * waves), BOTH, 0, 0)

    lines = lines.reshape(devices, 2, width, 2, bands, half).transpose(0, 4, 1, 5, 3, 2)
    uneven = np.full((lead, half), 2.0 / length)
    uneven[0, 0] = 1.0 / length
    speeds = tail_product(
        tail_inverse(length, lead, uneven), lines.reshape(lead, 2 * half, 2 * width)
    )
    last = -head_back[:, 1].reshape(lead, 2 * lead)
    speeds = head_product(last, speeds.reshape(2 * lead, tail, 2 * width))
    first = speeds[..., :width].reshape(length, width)
    second = speeds[..., width:].reshape(length, width)

    halo = []
    for cells in (field, first, second):
        halo.extend(edges(cells))
    halo = jnp.stack(halo, axis=-1)
    force = FORCE_AMP * np.cos(2.0 * np.pi * FORCE_WAVES / length * np.arange(length))
    force = jnp.asarray(force, jnp.float32)[:, None]
    rate = stencil(field, first, second, halo, force, closure_kernel)

    rate = lax.all_to_all(rate.reshape(parts, columns, width), "gy", 0, 0)
    return rate.swapaxes(1, 2).reshape(rows, columns)


def solution(mesh):
    placed = (P("gx", "gy"), P())
    return jax.shard_map(
        per_device, mesh=mesh, in_specs=placed, out_specs=P("gx", "gy"), check_vma=False
    )
```

```python
import functools
import math

import jax
import jax.numpy as jnp
import numpy as np
from jax import lax
from jax.experimental import pallas as pl
from jax.experimental.pallas import tpu as pltpu
from jax.sharding import PartitionSpec as P

VISCOSITY = 0.5
DRAG = 0.1
FORCE_AMP = 1.0
FORCE_WAVES = 4.0
TAIL = 64
NEAR = lax.Precision.HIGH
BOTH = ("gx", "gy")


def turns(period, *indices):
    product = functools.reduce(lambda a, b: a * b, np.ix_(*indices)) % period
    return np.exp(2j * np.pi / period * product)


def real_form(table, out_axis, in_axis):
    rows = [
        np.stack([table.real, -table.imag], axis=in_axis),
        np.stack([table.imag, table.real], axis=in_axis),
    ]
    return np.stack(rows, axis=out_axis).astype(np.float32)


def head_forward(lead):
    return real_form(turns(lead, np.arange(lead), np.arange(lead)).conj(), 1, 1)


def tail_forward(length, lead, kept):
    tail = length // lead
    c, b, d = np.arange(lead), np.arange(tail), np.arange(kept)
    table = turns(tail, d, b)[None] * turns(length, c, b)[:, None, :]
    real = real_form(table.conj(), 1, 2)
    return real.reshape(lead, 2 * kept, 2 * tail)


def tail_inverse(length, lead, weights):
    tail = length // lead
    c, b, d = np.arange(lead), np.arange(tail), np.arange(weights.shape[1])
    table = turns(tail, b, d)[None] * turns(length, c, b)[:, :, None] * weights[:, None, :]
    real = real_form(table, 1, 2)
    return real.reshape(lead, 2 * tail, 2 * weights.shape[1])


def head_product(table, cells):
    return jnp.einsum("rh,hbk->rbk", table, cells, precision=NEAR)


def tail_product(table, cells):
    return jnp.einsum("cmn,cnk->cmk", table, cells, precision=NEAR)


def stencil_kernel(grid_length, weights, *refs):
    out_ref = refs[-1]
    rows = out_ref.shape[0]
    fields = [refs[3 * i : 3 * i + 3] for i in range(3)]
    halo = jnp.concatenate([ref[...] for ref in refs[9:12]], axis=0)
    turned = [None, None, None]
    shifted = []
    for channel in range(3):
        mid, before, after = fields[channel]
        centre = jnp.concatenate([before[...], mid[...], after[...]], axis=0)
        minus = jnp.concatenate([halo[:, 2 * channel : 2 * channel + 1], centre[:, :-1]], axis=1)
        plus = jnp.concatenate([centre[:, 1:], halo[:, 2 * channel + 1 : 2 * channel + 2]], axis=1)
        trio = (minus, centre, plus)
        shifted.append(trio)
        for shift_second in range(3):
            for shift_first in range(3):
                term = weights[channel * 9 + shift_first * 3 + shift_second] * trio[shift_first]
                known = turned[shift_second]
                turned[shift_second] = term if known is None else known + term
    closure = turned[0][7 : 7 + rows] + turned[1][8 : 8 + rows] + turned[2][9 : 9 + rows]
    x_minus, whole, x_plus = shifted[0]
    x_minus, x_plus = x_minus[8 : 8 + rows], x_plus[8 : 8 + rows]
    centre = whole[8 : 8 + rows]
    y_minus, y_plus = whole[7 : 7 + rows], whole[9 : 9 + rows]
    first, second = fields[1][0][...], fields[2][0][...]
    advect = jnp.maximum(first, 0.0) * (centre - x_minus) + jnp.minimum(first, 0.0) * (x_plus - centre)
    advect += jnp.maximum(second, 0.0) * (centre - y_minus) + jnp.minimum(second, 0.0) * (y_plus - centre)
    laplace = x_plus + x_minus + y_plus + y_minus - 4.0 * centre
    force = refs[12][...]
    out_ref[...] = closure - advect + VISCOSITY * laplace - DRAG * centre + force


def stencil(field, first, second, halo, force, closure_kernel):
    length, width = field.shape
    rows = 128
    steps = rows // 8
    last = length // 8

    def specs(columns):
        return [
            pl.BlockSpec((rows, columns), lambda i: (i, 0)),
            pl.BlockSpec((8, columns), lambda i: ((i * steps + last - 1) % last, 0)),
            pl.BlockSpec((8, columns), lambda i: ((i * steps + steps) % last, 0)),
        ]

    halo_specs = specs(halo.shape[1])

    def body(weights_ref, *refs):
        weights = [weights_ref[i] for i in range(27)]
        stencil_kernel(length, weights, *refs)

    return pl.pallas_call(
        body,
        grid=(length // rows,),
        in_specs=[pl.BlockSpec(memory_space=pltpu.SMEM)]
        + specs(width) * 3
        + [halo_specs[1], halo_specs[0], halo_specs[2]]
        + [pl.BlockSpec((rows, 1), lambda i: (i, 0))],
        out_specs=pl.BlockSpec((rows, width), lambda i: (i, 0)),
        out_shape=jax.ShapeDtypeStruct((length, width), jnp.float32),
        compiler_params=pltpu.CompilerParams(vmem_limit_bytes=32 * 1024 * 1024),
    )(closure_kernel.reshape(27), *([field] * 3), *([first] * 3), *([second] * 3), *([halo] * 3), force)


def edges(cells):
    count = lax.axis_size("gx") * lax.axis_size("gy")
    onward = [(i, (i + 1) % count) for i in range(count)]
    backward = [((i + 1) % count, i) for i in range(count)]
    from_left = lax.ppermute(cells[..., -1], BOTH, onward)
    from_right = lax.ppermute(cells[..., 0], BOTH, backward)
    return from_left, from_right


def per_device(vorticity, closure_kernel):
    parts = lax.axis_size("gy")
    devices = lax.axis_size("gx") * parts
    rows, columns = vorticity.shape
    length = columns * parts
    width = rows // parts
    tail = min(TAIL, width)
    lead = length // tail
    half = tail // 2
    bands = lead // devices
    waves = bands * half
    folds = width // tail

    turned = vorticity.reshape(parts, width, columns).swapaxes(1, 2)
    field = lax.all_to_all(turned, "gy", 0, 0).reshape(length, width)

    head = head_forward(lead)
    section = head_product(
        head[:, :, 0, :].reshape(2 * lead, lead), field.reshape(lead, tail, width)
    )
    section = tail_product(
        tail_forward(length, lead, half), section.reshape(lead, 2 * tail, width)
    )
    section = section.reshape(devices, bands, 2, half, width).transpose(0, 2, 4, 1, 3)
    lines = lax.all_to_all(section.reshape(devices, 2, width, waves), BOTH, 0, 0)

    mixed = head.reshape(lead, 2, 2, devices, folds).transpose(0, 1, 3, 2, 4)
    wave = head_product(
        mixed.reshape(2 * lead, 2 * lead), lines.reshape(2 * lead, tail, waves)
    )
    wave = tail_product(
        tail_forward(length, lead, tail), wave.reshape(lead, 2 * tail, waves)
    ).reshape(lead, 2, tail, waves)

    unit = 2.0 * math.pi / length
    mode = np.arange(lead)[:, None] + lead * np.arange(tail)[None, :]
    mode = np.where(mode < length // 2, mode, mode - length)
    number_first = jnp.asarray(unit * mode, jnp.float32)[:, :, None]
    local = lax.axis_index(BOTH) * bands + jnp.arange(waves, dtype=jnp.int32) // half
    number_second = unit * (local + lead * (jnp.arange(waves, dtype=jnp.int32) % half)).astype(jnp.float32)
    squared = number_first**2 + number_second**2
    positive = squared > 0.0
    inverse = jnp.where(positive, 1.0 / jnp.where(positive, squared, 1.0), 0.0)
    potential = wave * inverse[:, None]
    even = np.full((lead, tail), 1.0 / length)
    columns_table = tail_inverse(length, lead, even)
    head_back = head.reshape(lead, 2, 2, lead).transpose(3, 2, 0, 1)
    mixed_back = head_back.reshape(devices, folds, 2, lead, 2).transpose(0, 2, 1, 3, 4)
    mixed_back = mixed_back.reshape(2 * lead, 2 * lead)
    uneven = np.full((lead, half), 2.0 / length)
    uneven[0, 0] = 1.0 / length
    lines_table = tail_inverse(length, lead, uneven)
    last = -head_back[:, 1].reshape(lead, 2 * lead)
    sent = []
    for factor in (number_second, -number_first[:, None]):
        spectral = (potential * factor).reshape(lead, 2 * tail, waves)
        back = tail_product(columns_table, spectral)
        back = head_product(mixed_back, back.reshape(2 * lead, tail, waves))
        sent.append(lax.all_to_all(back.reshape(devices, 2, width, waves), BOTH, 0, 0))
    speeds = []
    for lines in sent:
        lines = lines.swapaxes(2, 3).reshape(devices, 2, bands, half, width).swapaxes(1, 2)
        speed = tail_product(lines_table, lines.reshape(lead, 2 * half, width))
        speed = head_product(last, speed.reshape(2 * lead, tail, width))
        speeds.append(speed.reshape(length, width))
    first, second = speeds

    halo = []
    for cells in (field, first, second):
        halo.extend(edges(cells))
    halo = jnp.stack(halo, axis=-1)
    force = FORCE_AMP * np.cos(2.0 * np.pi * FORCE_WAVES / length * np.arange(length))
    force = jnp.asarray(force, jnp.float32)[:, None]
    rate = stencil(field, first, second, halo, force, closure_kernel)

    rate = lax.all_to_all(rate.reshape(parts, columns, width), "gy", 0, 0)
    return rate.swapaxes(1, 2).reshape(rows, columns)


def solution(mesh):
    placed = (P("gx", "gy"), P())
    return jax.shard_map(
        per_device, mesh=mesh, in_specs=placed, out_specs=P("gx", "gy"), check_vma=False
    )
```
